32 devices in a mesh: gx: 4 (over y, x), gy: 8 (over z, core).
Axes of the slice: x: 2, y: 2, z: 4, core: 2. Of those that a mesh axis runs over, the one named last changes fastest.
Arguments:
- u_face: float32 [8, 2048, 2048], P(None, 'gy', 'gx'), may hold values from -6 to 6
- v_face: float32 [8, 2048, 2048], P(None, 'gy', 'gx'), may hold values from -6 to 6
- w_face: float32 [8, 2048, 2048], P(None, 'gy', 'gx'), may hold values from -6 to 6
- theta_field: float32 [8, 2048, 2048], P(None, 'gy', 'gx'), may hold values from -6 to 6
- density: float32 [8], replicated, may hold values from 0.3 to 1.5
- thickness: float32 [8], replicated, may hold values from 4 to 32
Outputs:
- u_new: float32 [8, 2048, 2048], P(None, 'gy', 'gx')
- v_new: float32 [8, 2048, 2048], P(None, 'gy', 'gx')
- w_new: float32 [8, 2048, 2048], P(None, 'gy', 'gx')
- theta_new: float32 [8, 2048, 2048], P(None, 'gy', 'gx')
- pressure: float32 [8, 2048, 2048], P(None, 'gy', 'gx')
The draws below stay inside these ranges and needn't reach their ends.
All inputs are finite; a program needn't handle non-finite values.
Results may differ from the reference program's by a relative error of at most 0.0003.
Values sent between devices are 32-bit elements; how exact they have to be, the bound alone decides.
No kernel may reach another device: no remote copies, remote signals or barrier semaphores. Data moves between devices by JAX's collectives and lax.ppermute only.
A program may use at most 192 MiB of HBM per device.

```python
import math
import jax
import jax.numpy as jnp

NX = 2048
NY = 2048
NZ = 8


def draw_w_face(key, part):
    values = jnp.clip(jax.random.normal(key, (NZ, NY, NX), jnp.float32), -6.0, 6.0)
    return values


def block_levels(rng, extent, shards, least, top_value):
    loudness = 1.0
    for axis_at, blocks in shards:
        draws = jax.random.uniform(jax.random.fold_in(jax.random.fold_in(rng, 6), axis_at), (blocks,), jnp.float32, least / len(shards), top_value / len(shards))
        loudness = loudness * jnp.repeat(jnp.exp(draws), extent[axis_at] // blocks).reshape((-1,) + (1,) * (len(extent) - 1 - axis_at))
    return loudness


def scatter_about(key, dims, scale, most, pieces=(), kind=jnp.bfloat16):
    factor_of = block_levels(key, dims, pieces, -0.22, 0.18) if pieces else 1.0
    result = jax.random.normal(key, dims, jnp.float32) * scale * factor_of
    return jnp.minimum(jnp.maximum(result, -most), most).astype(kind)


def setup_inputs(seed: int = 0) -> dict:
    splits = jax.random.split(jax.random.key(seed), 7)
    u_face = scatter_about(splits[0], (NZ, NY, NX), 1.0, 6.0, ((1, 8), (2, 4)), jnp.float32)
    v_face = scatter_about(splits[1], (NZ, NY, NX), 1.0, 6.0, ((1, 8), (2, 4)), jnp.float32)
    w_face = draw_w_face(jax.random.fold_in(splits[6], 71), 0)
    theta_field = scatter_about(splits[3], (NZ, NY, NX), 1.0, 6.0, ((1, 8), (2, 4)), jnp.float32)
    density = jnp.clip(jnp.exp(jax.random.uniform(splits[4], (NZ,), jnp.float32, math.log(0.3), math.log(1.5))), 0.3, 1.5)
    thickness = jnp.clip(jnp.exp(jax.random.uniform(splits[5], (NZ,), jnp.float32, math.log(4.0), math.log(32.0))), 4.0, 32.0)
    return dict(u_face=u_face, v_face=v_face, w_face=w_face, theta_field=theta_field, density=density, thickness=thickness)


time_step = 0.2
buoyancy_gain = 1.0


def lift_level(field):
    return jnp.concatenate([field[1:], field[-1:]], axis=0)


def upwind_flux(q_m2, q_m1, q_zero, q_p1, q_p2, q_p3, velocity):
    centred = velocity * (37.0 * (q_zero + q_p1) - 8.0 * (q_m1 + q_p2) + (q_m2 + q_p3)) / 60.0
    damped = jnp.abs(velocity) * (10.0 * (q_p1 - q_zero) - 5.0 * (q_p2 - q_m1) + (q_p3 - q_m2)) / 60.0
    return centred - damped


def vertical_tend(tracer, velocity, rho_face, rho_level, spacing):
    levels = tracer.shape[0]
    padded = jnp.pad(tracer, ((2, 3), (0, 0), (0, 0)), mode="edge")
    parts = [padded[2 + offset:2 + offset + levels] for offset in range(-2, 4)]
    flux_z = upwind_flux(*parts, velocity) * rho_face[:, None, None]
    below = jnp.concatenate([jnp.zeros_like(flux_z[:1]), flux_z[:-1]], axis=0)
    return -(flux_z - below) / (rho_level * spacing)[:, None, None]


def horizontal_tend(tracer, u_vel, v_vel):
    parts_x = [jnp.roll(tracer, -offset, axis=2) for offset in range(-2, 4)]
    flux_x = upwind_flux(*parts_x, u_vel)
    parts_y = [jnp.roll(tracer, -offset, axis=1) for offset in range(-2, 4)]
    flux_y = upwind_flux(*parts_y, v_vel)
    return -(flux_x - jnp.roll(flux_x, 1, axis=2)) - (flux_y - jnp.roll(flux_y, 1, axis=1))


def hartley(field, axis):
    spectrum = jnp.fft.fft(field, axis=axis)
    return jnp.real(spectrum) - jnp.imag(spectrum)


def tridiag_solve(lower_coef, upper_coef, eigen_sum, source_term):
    levels = source_term.shape[0]
    shape_b = (levels,) + (1,) * (source_term.ndim - 1)
    low_b = lower_coef.reshape(shape_b)
    high_b = upper_coef.reshape(shape_b)
    ratios = []
    partial_sols = []
    for level in range(levels):
        pivots = eigen_sum - low_b[level] - high_b[level]
        numerator = source_term[level]
        if level > 0:
            pivots = pivots - low_b[level] * ratios[-1]
            numerator = numerator - low_b[level] * partial_sols[-1]
        ratios.append(high_b[level] / pivots)
        partial_sols.append(numerator / pivots)
    solved_levels = [partial_sols[-1]]
    for level in range(levels - 2, -1, -1):
        solved_levels.append(partial_sols[level] - ratios[level] * solved_levels[-1])
    return jnp.stack(solved_levels[::-1], axis=0)


def eigen_line(indices, count):
    return -4.0 * jnp.sin(math.pi * indices / count) ** 2


def reference(u_face, v_face, w_face, theta_field, density, thickness):
    face_density = (density + lift_level(density)) / 2.0
    face_spacing = (thickness + lift_level(thickness)) / 2.0
    adv_theta = horizontal_tend(theta_field, u_face, v_face) + vertical_tend(theta_field, w_face, face_density, density, thickness)
    u_level = (u_face + lift_level(u_face)) / 2.0
    v_level = (v_face + lift_level(v_face)) / 2.0
    w_level = (w_face + lift_level(w_face)) / 2.0
    adv_w = horizontal_tend(w_face, u_level, v_level) + vertical_tend(w_face, w_level, lift_level(density), face_density, face_spacing)
    theta_new = theta_field + time_step * adv_theta
    w_star = w_face + time_step * (adv_w + buoyancy_gain * (theta_field + lift_level(theta_field)) / 2.0)
    mass_flux = face_density[:, None, None] * w_star
    mass_below = jnp.concatenate([jnp.zeros_like(mass_flux[:1]), mass_flux[:-1]], axis=0)
    divergence = (u_face - jnp.roll(u_face, 1, axis=2)) + (v_face - jnp.roll(v_face, 1, axis=1))
    divergence = divergence + (mass_flux - mass_below) / (density * thickness)[:, None, None]
    source_term = divergence / time_step
    spectra = hartley(hartley(source_term, 2), 1)
    eig_x = eigen_line(jnp.arange(NX, dtype=jnp.int32), NX)
    eig_y = eigen_line(jnp.arange(NY, dtype=jnp.int32), NY)
    eigen_sum = eig_y[:, None] + eig_x[None, :]
    lower_coef = jnp.concatenate([jnp.zeros((1,), density.dtype), face_density[:-1] / (density[1:] * thickness[1:] * face_spacing[:-1])])
    upper_coef = face_density / (density * thickness * face_spacing)
    solution = tridiag_solve(lower_coef, upper_coef, eigen_sum, spectra)
    pressure = hartley(hartley(solution, 1), 2) / (NX * NY)
    u_new = u_face - time_step * (jnp.roll(pressure, -1, axis=2) - pressure)
    v_new = v_face - time_step * (jnp.roll(pressure, -1, axis=1) - pressure)
    above = jnp.concatenate([pressure[1:], jnp.zeros_like(pressure[:1])], axis=0)
    w_new = w_star - time_step * (above - pressure) / face_spacing[:, None, None]
    return (u_new, v_new, w_new, theta_new, pressure)
```

```python
import math

import jax
import jax.numpy as jnp
import numpy as np
from jax import lax
from jax.experimental import pallas as pl
from jax.experimental.pallas import tpu as pltpu
from jax.sharding import PartitionSpec as P

time_step = 0.2
buoyancy_gain = 1.0


def from_behind(value, axis, steps):
    count = lax.axis_size(axis)
    pairs = [(source, (source + steps) % count) for source in range(count)]
    return lax.ppermute(value, axis, pairs)


def extended(value, sides, width):
    for axis, dim in sides:
        size, length = (lax.axis_size(axis), value.shape[dim])
        up = [(i, (i + 1) % size) for i in range(size)]
        down = [(j, i) for i, j in up]
        last = lax.slice_in_dim(value, length - width, length, axis=dim)
        first = lax.slice_in_dim(value, 0, width, axis=dim)
        before = lax.ppermute(last, axis, up)
        after = lax.ppermute(first, axis, down)
        value = jnp.concatenate([before, value, after], axis=dim)
    return value


def lift_level(field):
    return jnp.concatenate([field[1:], field[-1:]], axis=0)


def upwind_flux(q_m2, q_m1, q_zero, q_p1, q_p2, q_p3, velocity):
    centred = velocity * (37.0 * (q_zero + q_p1) - 8.0 * (q_m1 + q_p2) + (q_m2 + q_p3)) / 60.0
    damped = (
        jnp.abs(velocity) * (10.0 * (q_p1 - q_zero) - 5.0 * (q_p2 - q_m1) + (q_p3 - q_m2)) / 60.0
    )
    return centred - damped


def vertical_tend(tracer, velocity, rho_face, rho_level, spacing):
    levels = tracer.shape[0]
    padded = jnp.pad(tracer, ((2, 3), (0, 0), (0, 0)), mode="edge")
    parts = [padded[2 + offset : 2 + offset + levels] for offset in range(-2, 4)]
    flux_z = upwind_flux(*parts, velocity) * rho_face[:, None, None]
    below = jnp.concatenate([jnp.zeros_like(flux_z[:1]), flux_z[:-1]], axis=0)
    return -(flux_z - below) / (rho_level * spacing)[:, None, None]


def horizontal_local(tracer_rim, u_rim, v_rim, rows_y, cols_x):
    row_band = tracer_rim[:, 3 : 3 + rows_y, :]
    parts_x = [row_band[:, :, 2 + offset : 3 + offset + cols_x] for offset in range(-2, 4)]
    flux_x = upwind_flux(*parts_x, u_rim[:, 3 : 3 + rows_y, 2 : 3 + cols_x])
    col_band = tracer_rim[:, :, 3 : 3 + cols_x]
    parts_y = [col_band[:, 2 + offset : 3 + offset + rows_y, :] for offset in range(-2, 4)]
    flux_y = upwind_flux(*parts_y, v_rim[:, 2 : 3 + rows_y, 3 : 3 + cols_x])
    return -(flux_x[:, :, 1:] - flux_x[:, :, :-1]) - (flux_y[:, 1:, :] - flux_y[:, :-1, :])


high = lax.Precision.HIGHEST
vmem_bytes = 48 * 1024 * 1024
jacobi_sweeps = 8


def power(base, exponent):
    result = None
    while exponent:
        if exponent & 1:
            result = base if result is None else result * base
        exponent >>= 1
        if exponent:
            base = base * base
    return result


def jacobi_kernel(columns_ref, basis_ref, square_ref):
    levels = columns_ref.shape[0]
    rows = lax.broadcasted_iota(jnp.int32, columns_ref.shape[1:], 0)

    def sweep(_, state):
        factor, basis = list(state[0]), list(state[1])
        order = list(range(levels))
        for _round in range(levels - 1):
            for slot in range(levels // 2):
                i, j = sorted((order[slot], order[levels - 1 - slot]))
                norm_i = jnp.sum(factor[i] * factor[i], axis=0, keepdims=True)
                norm_j = jnp.sum(factor[j] * factor[j], axis=0, keepdims=True)
                cross = jnp.sum(factor[i] * factor[j], axis=0, keepdims=True)
                gap = norm_j - norm_i
                size = jnp.abs(gap) + jnp.sqrt(gap * gap + 4.0 * cross * cross)
                twice = jnp.where(gap < 0.0, -2.0 * cross, 2.0 * cross)
                tangent = jnp.where(size > 0.0, twice / jnp.where(size > 0.0, size, 1.0), 0.0)
                cosine = 1.0 / jnp.sqrt(1.0 + tangent * tangent)
                sine = cosine * tangent
                for held in (factor, basis):
                    left, right = held[i], held[j]
                    held[i] = cosine * left - sine * right
                    held[j] = sine * left + cosine * right
            order = [order[0], order[-1]] + order[1:-1]
        return tuple(factor), tuple(basis)

    start = (
        tuple(columns_ref[i] for i in range(levels)),
        tuple(jnp.where(rows == i, 1.0, 0.0) for i in range(levels)),
    )
    factor, basis = lax.fori_loop(0, jacobi_sweeps, sweep, start)
    for i in range(levels):
        basis_ref[i] = basis[i]
        square_ref[i] = jnp.broadcast_to(
            jnp.sum(factor[i] * factor[i], axis=0, keepdims=True), columns_ref.shape[1:]
        )


def vertical_modes(density, thickness, face_density, face_spacing):
    levels = density.shape[0]
    mass = density * thickness
    stiff = face_density / face_spacing
    diagonal = -jnp.sqrt(stiff / mass)
    beside = jnp.sqrt(stiff / jnp.concatenate([mass[1:], mass[-1:]]))
    factor = diagonal[:, None] * np.eye(levels, dtype=np.float32)
    factor = factor + beside[:, None] * np.eye(levels, k=1, dtype=np.float32)
    shape = jax.ShapeDtypeStruct((levels, levels, 128), jnp.float32)
    basis, square = pl.pallas_call(
        jacobi_kernel, out_shape=(shape, shape), name="vertical_modes"
    )(jnp.broadcast_to(factor.T[:, :, None], shape.shape))
    root_mass = jnp.sqrt(mass)[None, :]
    return basis[:, :, 0] * root_mass, basis[:, :, 0] / root_mass, square[:, 0, 0]


def decay_of(excess):
    return 1.0 / (1.0 + 0.5 * excess + jnp.sqrt(excess + 0.25 * excess * excess))


def sine_matrix(count):
    index = np.arange(count)
    matrix = np.sqrt(2.0 / count) * np.sin(np.pi * np.outer(index, index) % (2 * np.pi * count) / count)
    matrix[0, 0] = 1.0
    return matrix.astype(np.float32)


def edge_weights(count):
    matrix = sine_matrix(count)
    weights = np.zeros((count, 128), np.float32)
    weights[1:, 0] = matrix[1, 1:]
    weights[1:, 1] = matrix[count - 1, 1:]
    return weights


def run_sweeps(source, decay_ref, start_ref, work_ref, ends_ref, rows, levels):
    decay = decay_ref[...]

    def forward(j, carry):
        at = pl.ds(pl.multiple_of(j * levels, levels), levels)
        value = carry + source(at)
        scaled = decay * value
        work_ref[at, :] = scaled
        return scaled

    last = lax.fori_loop(0, rows, forward, jnp.zeros_like(decay), unroll=4)
    top = start_ref[...] * last
    ends_ref[0] = top
    work_ref[pl.ds((rows - 1) * levels, levels), :] = top

    def backward(step, carry):
        at = pl.ds(pl.multiple_of((rows - 2 - step) * levels, levels), levels)
        value = decay * carry - work_ref[at, :]
        work_ref[at, :] = value
        return value

    ends_ref[1] = lax.fori_loop(0, rows - 1, backward, top, unroll=4)


def first_kernel(modes_ref, sine_ref, weight_ref, decay_ref, start_ref, spectral_ref, edge_ref, ends_ref, work_ref):
    total, count = modes_ref.shape
    levels = decay_ref.shape[0]
    chunk = min(256, total)

    @pl.loop(0, total // chunk)
    def _(step):
        at = pl.ds(pl.multiple_of(step * chunk, chunk), chunk)
        spectral_ref[at, :] = jnp.dot(modes_ref[at, :], sine_ref[...], precision=high)

    run_sweeps(lambda at: spectral_ref[at, :], decay_ref, start_ref, work_ref, ends_ref, total // levels, levels)

    @pl.loop(0, total // chunk)
    def _(step):
        at = pl.ds(pl.multiple_of(step * chunk, chunk), chunk)
        lane = lax.broadcasted_iota(jnp.int32, (chunk, 128), 1)
        near = jnp.where(lane == 0, spectral_ref[at, 0:128], 0.0)
        edge_ref[at, :] = near - jnp.dot(work_ref[at, :], weight_ref[...], precision=high)


def coupled_terms(decay_ref, ends_ref, work_ref, rows, levels):
    decay = decay_ref[...]

    def upward(j, carry):
        at = pl.ds(pl.multiple_of(j * levels, levels), levels)
        value = decay * carry
        work_ref[at, :] += value
        return value

    lax.fori_loop(0, rows, upward, ends_ref[0], unroll=4)

    def downward(step, carry):
        at = pl.ds(pl.multiple_of((rows - 1 - step) * levels, levels), levels)
        value = decay * carry
        work_ref[at, :] += value
        return value

    lax.fori_loop(0, rows, downward, ends_ref[1], unroll=4)


def second_kernel(decay_ref, ends_ref, weight_ref, edge_in_ref, edge_ref, work_ref):
    total, _ = work_ref.shape
    levels = decay_ref.shape[0]
    chunk = min(256, total)
    work_ref[...] = jnp.zeros_like(work_ref)
    coupled_terms(decay_ref, ends_ref, work_ref, total // levels, levels)

    @pl.loop(0, total // chunk)
    def _(step):
        at = pl.ds(pl.multiple_of(step * chunk, chunk), chunk)
        edge_ref[at, :] = edge_in_ref[at, :] - jnp.dot(work_ref[at, :], weight_ref[...], precision=high)


def third_kernel(spectral_ref, line_ref, spread_ref, decay_ref, start_ref, free_ref, ends_ref, work_ref):
    total, _ = spectral_ref.shape
    levels = decay_ref.shape[0]
    chunk = min(256, total)

    @pl.loop(0, total // chunk)
    def _(step):
        at = pl.ds(pl.multiple_of(step * chunk, chunk), chunk)
        work_ref[at, :] = spectral_ref[at, :] - jnp.dot(line_ref[at, :], spread_ref[...], precision=high)

    run_sweeps(lambda at: work_ref[at, :], decay_ref, start_ref, free_ref, ends_ref, total // levels, levels)


def fourth_kernel(free_ref, line_ref, sine_ref, decay_ref, ends_ref, out_ref, work_ref):
    total, count = free_ref.shape
    levels = decay_ref.shape[0]
    chunk = min(256, total)
    work_ref[...] = free_ref[...]
    coupled_terms(decay_ref, ends_ref, work_ref, total // levels, levels)

    @pl.loop(0, total // chunk)
    def _(step):
        at = pl.ds(pl.multiple_of(step * chunk, chunk), chunk)
        lane = lax.broadcasted_iota(jnp.int32, (chunk, count), 1)
        column = jnp.broadcast_to(line_ref[at, 0:1], (chunk, count))
        full = jnp.where(lane == 0, column, work_ref[at, :])
        out_ref[at, :] = jnp.dot(full, sine_ref[...], precision=high)


def couple(ends, ratio):
    groups, here = lax.axis_size("gy"), lax.axis_index("gy")
    gathered = lax.all_gather(ends, "gy")
    block = jnp.arange(groups, dtype=jnp.int32)
    scale = 1.0 / (1.0 - power(ratio, groups))

    def weighted(values, exponent):
        factor, base, bit = jnp.ones_like(values), ratio, 1
        while bit < groups:
            factor = jnp.where((exponent & bit)[:, None, None] > 0, factor * base, factor)
            base, bit = base * base, bit * 2
        return jnp.sum(values * factor, axis=0) * scale

    from_low = weighted(gathered[:, 0], (here - 1 - block + 2 * groups) % groups)
    from_high = weighted(gathered[:, 1], (block - here - 1 + 2 * groups) % groups)
    return jnp.stack([from_low, from_high])


def split_count(count):
    inner = 2 ** ((count.bit_length() - 1) // 2)
    return count // inner, inner


def twiddles(rows, cols, count):
    angles = 2.0 * np.pi * (np.outer(np.arange(rows), np.arange(cols)) % count) / count
    return np.cos(angles).astype(np.float32), np.sin(angles).astype(np.float32)


def hartley_lines(lines):
    count = lines.shape[-1]
    outer, inner = split_count(count)
    shaped = lines.reshape(lines.shape[:-1] + (outer, inner))
    cos_q, sin_q = twiddles(outer, outer, outer)
    cos_t, sin_t = twiddles(outer, inner, count)
    cos_p, sin_p = twiddles(inner, inner, inner)
    real = jnp.einsum("aqp,mq->amp", shaped, cos_q, precision=high)
    imag = -jnp.einsum("aqp,mq->amp", shaped, sin_q, precision=high)
    turned_re = real * cos_t + imag * sin_t
    turned_im = imag * cos_t - real * sin_t
    result = jnp.einsum("amp,pn->amn", turned_re, cos_p + sin_p, precision=high)
    return result + jnp.einsum("amp,pn->amn", turned_im, sin_p - cos_p, precision=high)


def hartley_back(spectra):
    outer, inner = spectra.shape[-2:]
    count = outer * inner
    cos_q, sin_q = twiddles(outer, outer, outer)
    cos_t, sin_t = twiddles(outer, inner, count)
    cos_p, sin_p = twiddles(inner, inner, inner)
    real = jnp.einsum("amn,np->amp", spectra, cos_p, precision=high)
    imag = -jnp.einsum("amn,np->amp", spectra, sin_p, precision=high)
    turned_re = real * cos_t + imag * sin_t
    turned_im = imag * cos_t - real * sin_t
    result = jnp.einsum("amp,qm->aqp", turned_re, cos_q + sin_q, precision=high)
    result = result + jnp.einsum("amp,qm->aqp", turned_im, sin_q - cos_q, precision=high)
    return result.reshape(spectra.shape[:-2] + (count,)) / count


def separator_solve(edge, square, rows, cols_x):
    groups_x, groups_y = lax.axis_size("gx"), lax.axis_size("gy")
    levels = square.shape[0]
    count = groups_y * rows
    sides = edge.reshape(rows, levels, 128)[:, :, :2].transpose(2, 1, 0)
    lines = lax.all_gather(sides, ("gx", "gy"))
    lines = lines.reshape(groups_x, groups_y, 2, levels, rows).transpose(2, 0, 3, 1, 4)
    residual = (lines[0] + jnp.roll(lines[1], 1, axis=0)).reshape(groups_x * levels, count)
    spectra = hartley_lines(residual)
    outer, inner = split_count(count)
    index = np.arange(outer)[:, None] + outer * np.arange(inner)[None, :]
    excess = (4.0 * np.sin(np.pi * index / count) ** 2).astype(np.float32) + square[:, None, None]
    ratio = power(decay_of(excess), cols_x)
    scale = -1.0 / ((1.0 - power(ratio, groups_x)) * jnp.sqrt(excess * (excess + 4.0)))
    powers = [jnp.ones_like(ratio)]
    for _ in range(groups_x):
        powers.append(powers[-1] * ratio)
    here = lax.axis_index("gx")
    spectra = spectra.reshape(groups_x, levels, outer, inner)
    twice = jnp.concatenate([spectra, spectra, spectra[:1]], axis=0)
    ahead = lax.dynamic_slice_in_dim(twice, here, groups_x + 1, axis=0)
    own = sum((powers[d] + powers[groups_x - d]) * ahead[d] for d in range(groups_x))
    east = sum((powers[d] + powers[groups_x - d]) * ahead[d + 1] for d in range(groups_x))
    solved = jnp.stack([own * scale, east * scale]).reshape(2 * levels, outer, inner)
    whole = hartley_back(solved).reshape(2, levels, count)
    mine = lax.dynamic_slice_in_dim(whole, lax.axis_index("gy") * rows, rows, axis=2)
    flat = mine.transpose(2, 1, 0).reshape(rows * levels, 2)
    return jnp.pad(flat, ((0, 0), (0, 126)))


def pressure_modes(modes, square):
    total, cols_x = modes.shape
    levels = square.shape[0]
    rows = total // levels
    sine = sine_matrix(cols_x)
    weight = edge_weights(cols_x)
    index = np.arange(cols_x)
    excess = (4.0 * np.sin(np.pi * index / (2 * cols_x)) ** 2).astype(np.float32) + square[:, None]
    decay = jnp.where(index[None, :] > 0, decay_of(excess), 0.0)
    start = -1.0 / (1.0 - decay * decay)
    ratio = power(decay, rows)
    big = jax.ShapeDtypeStruct((total, cols_x), jnp.float32)
    strip = jax.ShapeDtypeStruct((total, 128), jnp.float32)
    ends = jax.ShapeDtypeStruct((2, levels, cols_x), jnp.float32)
    scratch = [pltpu.VMEM((total, cols_x), jnp.float32)]
    params = pltpu.CompilerParams(vmem_limit_bytes=vmem_bytes)

    def call(kernel, outs, name):
        return pl.pallas_call(kernel, out_shape=outs, scratch_shapes=scratch, compiler_params=params, name=name)

    spectral, edge, free_ends = call(first_kernel, (big, strip, ends), "first_solve")(
        modes, sine, weight, decay, start
    )
    edge = call(second_kernel, strip, "edge_terms")(decay, couple(free_ends, ratio), weight, edge)
    lines = separator_solve(edge, square, rows, cols_x)
    free, free_ends = call(third_kernel, (big, ends), "second_solve")(
        spectral, lines, weight.T, decay, start
    )
    return call(fourth_kernel, big, "to_columns")(free, lines, sine, decay, couple(free_ends, ratio))


def shift_gradient(pressure):
    east_cells = from_behind(pressure[:, :, :1], "gx", -1)
    north_cells = from_behind(pressure[:, :1, :], "gy", -1)
    grad_x = jnp.concatenate([pressure[:, :, 1:], east_cells], axis=2) - pressure
    grad_y = jnp.concatenate([pressure[:, 1:, :], north_cells], axis=1) - pressure
    return (grad_x, grad_y)


def per_device(u_face, v_face, w_face, theta_field, density, thickness):
    levels, rows_y, cols_x = theta_field.shape
    theta_rim, w_rim, u_rim, v_rim = (
        extended(theta_field, (("gx", 2), ("gy", 1)), 3),
        extended(w_face, (("gx", 2), ("gy", 1)), 3),
        extended(u_face, (("gx", 2), ("gy", 1)), 3),
        extended(v_face, (("gx", 2), ("gy", 1)), 3),
    )
    face_density = (density + lift_level(density)) / 2.0
    face_spacing = (thickness + lift_level(thickness)) / 2.0
    forward, back, square = vertical_modes(density, thickness, face_density, face_spacing)
    adv_theta = horizontal_local(theta_rim, u_rim, v_rim, rows_y, cols_x) + vertical_tend(
        theta_field, w_face, face_density, density, thickness
    )
    u_level = (u_rim + lift_level(u_rim)) / 2.0
    v_level = (v_rim + lift_level(v_rim)) / 2.0
    w_level = (w_face + lift_level(w_face)) / 2.0
    adv_w = horizontal_local(w_rim, u_level, v_level, rows_y, cols_x) + vertical_tend(
        w_face, w_level, lift_level(density), face_density, face_spacing
    )
    theta_new = theta_field + time_step * adv_theta
    w_star = w_face + time_step * (
        adv_w + buoyancy_gain * (theta_field + lift_level(theta_field)) / 2.0
    )
    mass_flux = face_density[:, None, None] * w_star
    mass_below = jnp.concatenate([jnp.zeros_like(mass_flux[:1]), mass_flux[:-1]], axis=0)
    divergence = (
        u_face
        - u_rim[:, 3 : 3 + rows_y, 2 : 2 + cols_x]
        + (v_face - v_rim[:, 2 : 2 + rows_y, 3 : 3 + cols_x])
    )
    divergence = divergence + (mass_flux - mass_below) / (density * thickness)[:, None, None]
    source_term = divergence / time_step
    modes = jnp.einsum("kl,lyx->ykx", forward, source_term, precision=high)
    solved = pressure_modes(modes.reshape(rows_y * levels, cols_x), square)
    pressure = jnp.einsum("kl,ykx->lyx", back, solved.reshape(rows_y, levels, cols_x), precision=high)
    grad_x, grad_y = shift_gradient(pressure)
    u_new = u_face - time_step * grad_x
    v_new = v_face - time_step * grad_y
    above = jnp.concatenate([pressure[1:], jnp.zeros_like(pressure[:1])], axis=0)
    w_new = w_star - time_step * (above - pressure) / face_spacing[:, None, None]
    return (u_new, v_new, w_new, theta_new, pressure)


def solution(mesh):
    blocks = P(None, "gy", "gx")
    return jax.shard_map(
        per_device,
        mesh=mesh,
        in_specs=(blocks, blocks, blocks, blocks, P(), P()),
        out_specs=(blocks,) * 5,
        check_vma=False,
    )
```

```python
import math

import jax
import jax.numpy as jnp
import numpy as np
from jax import lax
from jax.experimental import pallas as pl
from jax.experimental.pallas import tpu as pltpu
from jax.sharding import PartitionSpec as P

time_step = 0.2
buoyancy_gain = 1.0


def from_behind(value, axis, steps):
    count = lax.axis_size(axis)
    pairs = [(source, (source + steps) % count) for source in range(count)]
    return lax.ppermute(value, axis, pairs)


def lift_level(field):
    return jnp.concatenate([field[1:], field[-1:]], axis=0)


high = lax.Precision.HIGHEST
vmem_bytes = 48 * 1024 * 1024
jacobi_sweeps = 8


def power(base, exponent):
    result = None
    while exponent:
        if exponent & 1:
            result = base if result is None else result * base
        exponent >>= 1
        if exponent:
            base = base * base
    return result


def jacobi_kernel(columns_ref, basis_ref, square_ref):
    levels = columns_ref.shape[0]
    rows = lax.broadcasted_iota(jnp.int32, columns_ref.shape[1:], 0)

    def sweep(_, state):
        factor, basis = list(state[0]), list(state[1])
        order = list(range(levels))
        for _round in range(levels - 1):
            for slot in range(levels // 2):
                i, j = sorted((order[slot], order[levels - 1 - slot]))
                norm_i = jnp.sum(factor[i] * factor[i], axis=0, keepdims=True)
                norm_j = jnp.sum(factor[j] * factor[j], axis=0, keepdims=True)
                cross = jnp.sum(factor[i] * factor[j], axis=0, keepdims=True)
                gap = norm_j - norm_i
                size = jnp.abs(gap) + jnp.sqrt(gap * gap + 4.0 * cross * cross)
                twice = jnp.where(gap < 0.0, -2.0 * cross, 2.0 * cross)
                tangent = jnp.where(size > 0.0, twice / jnp.where(size > 0.0, size, 1.0), 0.0)
                cosine = 1.0 / jnp.sqrt(1.0 + tangent * tangent)
                sine = cosine * tangent
                for held in (factor, basis):
                    left, right = held[i], held[j]
                    held[i] = cosine * left - sine * right
                    held[j] = sine * left + cosine * right
            order = [order[0], order[-1]] + order[1:-1]
        return tuple(factor), tuple(basis)

    start = (
        tuple(columns_ref[i] for i in range(levels)),
        tuple(jnp.where(rows == i, 1.0, 0.0) for i in range(levels)),
    )
    factor, basis = lax.fori_loop(0, jacobi_sweeps, sweep, start)
    for i in range(levels):
        basis_ref[i] = basis[i]
        square_ref[i] = jnp.broadcast_to(
            jnp.sum(factor[i] * factor[i], axis=0, keepdims=True), columns_ref.shape[1:]
        )


def vertical_modes(density, thickness, face_density, face_spacing):
    levels = density.shape[0]
    mass = density * thickness
    stiff = face_density / face_spacing
    diagonal = -jnp.sqrt(stiff / mass)
    beside = jnp.sqrt(stiff / jnp.concatenate([mass[1:], mass[-1:]]))
    factor = diagonal[:, None] * np.eye(levels, dtype=np.float32)
    factor = factor + beside[:, None] * np.eye(levels, k=1, dtype=np.float32)
    shape = jax.ShapeDtypeStruct((levels, levels, 128), jnp.float32)
    basis, square = pl.pallas_call(
        jacobi_kernel, out_shape=(shape, shape), name="vertical_modes"
    )(jnp.broadcast_to(factor.T[:, :, None], shape.shape))
    root_mass = jnp.sqrt(mass)[None, :]
    return basis[:, :, 0] * root_mass, basis[:, :, 0] / root_mass, square[:, 0, 0]


def decay_of(excess):
    return 1.0 / (1.0 + 0.5 * excess + jnp.sqrt(excess + 0.25 * excess * excess))


def sine_matrix(count):
    index = np.arange(count)
    matrix = np.sqrt(2.0 / count) * np.sin(np.pi * np.outer(index, index) % (2 * np.pi * count) / count)
    matrix[0, 0] = 1.0
    return matrix.astype(np.float32)


def edge_weights(count):
    matrix = sine_matrix(count)
    weights = np.zeros((count, 128), np.float32)
    weights[1:, 0] = matrix[1, 1:]
    weights[1:, 1] = matrix[count - 1, 1:]
    return weights


def row_of(j, levels):
    return pl.ds(pl.multiple_of(j * levels, levels), levels)


def forward_rows(source, decay, work_ref, first, rows, carry):
    levels = decay.shape[0]

    def step(j, carry):
        scaled = decay * (carry + source(j))
        work_ref[row_of(first + j, levels), :] = scaled
        return scaled

    return lax.fori_loop(0, rows, step, carry, unroll=4)


def backward_rows(last, decay, start, work_ref, ends_ref, rows):
    levels = decay.shape[0]
    top = start * last
    ends_ref[0] = top
    work_ref[row_of(rows - 1, levels), :] = top

    def step(j, carry):
        at = row_of(rows - 2 - j, levels)
        value = decay * carry - work_ref[at, :]
        work_ref[at, :] = value
        return value

    ends_ref[1] = lax.fori_loop(0, rows - 1, step, top, unroll=4)


def coupled_terms(decay_ref, ends_ref, work_ref, rows, levels):
    decay = decay_ref[...]

    def upward(j, carry):
        at = pl.ds(pl.multiple_of(j * levels, levels), levels)
        value = decay * carry
        work_ref[at, :] += value
        return value

    lax.fori_loop(0, rows, upward, ends_ref[0], unroll=4)

    def downward(step, carry):
        at = pl.ds(pl.multiple_of((rows - 1 - step) * levels, levels), levels)
        value = decay * carry
        work_ref[at, :] += value
        return value

    lax.fori_loop(0, rows, downward, ends_ref[1], unroll=4)


def second_kernel(decay_ref, ends_ref, weight_ref, edge_in_ref, edge_ref, work_ref):
    total, _ = work_ref.shape
    levels = decay_ref.shape[0]
    chunk = min(256, total)
    work_ref[...] = jnp.zeros_like(work_ref)
    coupled_terms(decay_ref, ends_ref, work_ref, total // levels, levels)

    @pl.loop(0, total // chunk)
    def _(step):
        at = pl.ds(pl.multiple_of(step * chunk, chunk), chunk)
        edge_ref[at, :] = edge_in_ref[at, :] - jnp.dot(work_ref[at, :], weight_ref[...], precision=high)


def third_kernel(spectral_ref, line_ref, spread_ref, decay_ref, start_ref, free_ref, ends_ref, work_ref):
    total, _ = spectral_ref.shape
    levels = decay_ref.shape[0]
    chunk = min(256, total)

    @pl.loop(0, total // chunk)
    def _(step):
        at = pl.ds(pl.multiple_of(step * chunk, chunk), chunk)
        work_ref[at, :] = spectral_ref[at, :] - jnp.dot(line_ref[at, :], spread_ref[...], precision=high)

    decay, rows = decay_ref[...], total // levels
    last = forward_rows(
        lambda j: work_ref[row_of(j, levels), :], decay, free_ref, 0, rows, jnp.zeros_like(decay)
    )
    backward_rows(last, decay, start_ref[...], free_ref, ends_ref, rows)


def couple(ends, ratio):
    groups, here = lax.axis_size("gy"), lax.axis_index("gy")
    gathered = lax.all_gather(ends, "gy")
    block = jnp.arange(groups, dtype=jnp.int32)
    scale = 1.0 / (1.0 - power(ratio, groups))

    def weighted(values, exponent):
        factor, base, bit = jnp.ones_like(values), ratio, 1
        while bit < groups:
            factor = jnp.where((exponent & bit)[:, None, None] > 0, factor * base, factor)
            base, bit = base * base, bit * 2
        return jnp.sum(values * factor, axis=0) * scale

    from_low = weighted(gathered[:, 0], (here - 1 - block + 2 * groups) % groups)
    from_high = weighted(gathered[:, 1], (block - here - 1 + 2 * groups) % groups)
    return jnp.stack([from_low, from_high])


def split_count(count):
    inner = 2 ** ((count.bit_length() - 1) // 2)
    return count // inner, inner


def twiddles(rows, cols, count):
    angles = 2.0 * np.pi * (np.outer(np.arange(rows), np.arange(cols)) % count) / count
    return np.cos(angles).astype(np.float32), np.sin(angles).astype(np.float32)


def hartley_lines(lines):
    count = lines.shape[-1]
    outer, inner = split_count(count)
    shaped = lines.reshape(lines.shape[:-1] + (outer, inner))
    cos_q, sin_q = twiddles(outer, outer, outer)
    cos_t, sin_t = twiddles(outer, inner, count)
    cos_p, sin_p = twiddles(inner, inner, inner)
    real = jnp.einsum("aqp,mq->amp", shaped, cos_q, precision=high)
    imag = -jnp.einsum("aqp,mq->amp", shaped, sin_q, precision=high)
    turned_re = real * cos_t + imag * sin_t
    turned_im = imag * cos_t - real * sin_t
    result = jnp.einsum("amp,pn->amn", turned_re, cos_p + sin_p, precision=high)
    return result + jnp.einsum("amp,pn->amn", turned_im, sin_p - cos_p, precision=high)


def hartley_back(spectra):
    outer, inner = spectra.shape[-2:]
    count = outer * inner
    cos_q, sin_q = twiddles(outer, outer, outer)
    cos_t, sin_t = twiddles(outer, inner, count)
    cos_p, sin_p = twiddles(inner, inner, inner)
    real = jnp.einsum("amn,np->amp", spectra, cos_p, precision=high)
    imag = -jnp.einsum("amn,np->amp", spectra, sin_p, precision=high)
    turned_re = real * cos_t + imag * sin_t
    turned_im = imag * cos_t - real * sin_t
    result = jnp.einsum("amp,qm->aqp", turned_re, cos_q + sin_q, precision=high)
    result = result + jnp.einsum("amp,qm->aqp", turned_im, sin_q - cos_q, precision=high)
    return result.reshape(spectra.shape[:-2] + (count,)) / count


def separator_solve(edge, square, rows, cols_x):
    groups_x, groups_y = lax.axis_size("gx"), lax.axis_size("gy")
    levels = square.shape[0]
    count = groups_y * rows
    sides = edge.reshape(rows, levels, 128)[:, :, :2].transpose(2, 1, 0)
    lines = lax.all_gather(sides, ("gx", "gy"))
    lines = lines.reshape(groups_x, groups_y, 2, levels, rows).transpose(2, 0, 3, 1, 4)
    residual = (lines[0] + jnp.roll(lines[1], 1, axis=0)).reshape(groups_x * levels, count)
    spectra = hartley_lines(residual)
    outer, inner = split_count(count)
    index = np.arange(outer)[:, None] + outer * np.arange(inner)[None, :]
    excess = (4.0 * np.sin(np.pi * index / count) ** 2).astype(np.float32) + square[:, None, None]
    ratio = power(decay_of(excess), cols_x)
    scale = -1.0 / ((1.0 - power(ratio, groups_x)) * jnp.sqrt(excess * (excess + 4.0)))
    powers = [jnp.ones_like(ratio)]
    for _ in range(groups_x):
        powers.append(powers[-1] * ratio)
    here = lax.axis_index("gx")
    spectra = spectra.reshape(groups_x, levels, outer, inner)
    twice = jnp.concatenate([spectra, spectra, spectra[:1]], axis=0)
    ahead = lax.dynamic_slice_in_dim(twice, here, groups_x + 1, axis=0)
    own = sum((powers[d] + powers[groups_x - d]) * ahead[d] for d in range(groups_x))
    east = sum((powers[d] + powers[groups_x - d]) * ahead[d + 1] for d in range(groups_x))
    solved = jnp.stack([own * scale, east * scale]).reshape(2 * levels, outer, inner)
    whole = hartley_back(solved).reshape(2, levels, count)
    whole = jnp.concatenate([whole, whole[:, :, :1]], axis=2)
    mine = lax.dynamic_slice_in_dim(whole, lax.axis_index("gy") * rows, rows + 1, axis=2)
    flat = mine.transpose(2, 1, 0).reshape((rows + 1) * levels, 2)
    return jnp.pad(flat, ((0, 0), (0, 126)))


def upper_of(field):
    rolled = pltpu.roll(field, field.shape[0] - 1, 0)
    sub = lax.broadcasted_iota(jnp.int32, field.shape, 0)
    return jnp.where(sub == field.shape[0] - 1, field, rolled)


def lower_of(field):
    rolled = pltpu.roll(field, 1, 0)
    sub = lax.broadcasted_iota(jnp.int32, field.shape, 0)
    return jnp.where(sub == 0, field, rolled)


def zero_below(field):
    sub = lax.broadcasted_iota(jnp.int32, field.shape, 0)
    return jnp.where(sub == 0, 0.0, pltpu.roll(field, 1, 0))


def flux60(q_m2, q_m1, q_zero, q_p1, q_p2, q_p3, speed):
    centred = 37.0 * (q_zero + q_p1) - 8.0 * (q_m1 + q_p2) + (q_m2 + q_p3)
    damped = 10.0 * (q_p1 - q_zero) - 5.0 * (q_p2 - q_m1) + (q_p3 - q_m2)
    return speed * centred - jnp.abs(speed) * damped


def wide(tile, count):
    return jnp.concatenate([tile] * (count // tile.shape[1]), axis=1)


def mix_levels(field, mixer):
    total = mixer[0] * field
    for shift in range(1, field.shape[0]):
        total = total + mixer[shift] * pltpu.roll(field, shift, 0)
    return total


def pack_kernel(
    th_lo, th_hi, w_lo, w_hi, v_hi, th_left, th_right, w_left, w_right, u_right, north, south, east, west
):
    north[0] = jnp.concatenate([th_hi[0, 5:8], w_hi[0, 5:8], v_hi[0, 7:8], v_hi[0, 7:8]], axis=0)
    south[0] = jnp.concatenate([th_lo[0, 0:3], w_lo[0, 0:3], w_lo[0, 0:2]], axis=0)
    lane = lax.broadcasted_iota(jnp.int32, th_left.shape[1:], 1)
    merged = jnp.where(lane < 3, pltpu.roll(th_right[0], 3, 1), pltpu.roll(w_right[0], 6, 1))
    merged = jnp.where(lane < 6, merged, pltpu.roll(u_right[0], 7, 1))
    east[0] = merged.T[0:8, :]
    west[0] = jnp.where(lane < 3, th_left[0], pltpu.roll(w_left[0], 3, 1)).T[0:8, :]


def pack_sides(u_face, v_face, w_face, theta_field):
    levels, rows, cols = theta_field.shape
    low = pl.BlockSpec((1, 8, cols), lambda k: (k, 0, 0))
    top = pl.BlockSpec((1, 8, cols), lambda k: (k, rows // 8 - 1, 0))
    left = pl.BlockSpec((1, rows, 128), lambda k: (k, 0, 0))
    right = pl.BlockSpec((1, rows, 128), lambda k: (k, 0, cols // 128 - 1))
    flat = jax.ShapeDtypeStruct((levels, 8, cols), jnp.float32)
    tall = jax.ShapeDtypeStruct((levels, 8, rows), jnp.float32)
    tall_spec = pl.BlockSpec((1, 8, rows), lambda k: (k, 0, 0))
    return pl.pallas_call(
        pack_kernel,
        grid=(levels,),
        in_specs=[low, top, low, top, top, left, right, left, right, right],
        out_specs=(low, low, tall_spec, tall_spec),
        out_shape=(flat, flat, tall, tall),
        name="pack_sides",
    )(theta_field, theta_field, w_face, w_face, v_face, theta_field, theta_field, w_face, w_face, u_face)


def rim_lanes(west, east, own):
    flux_theta = flux60(*[west[:, f] for f in range(3)], *[own[:, f] for f in range(3)], west[:, 6] * (time_step / 60.0))
    u_sum = (west[:, 6] + lift_level(west[:, 6])) * (0.5 * time_step / 60.0)
    flux_w = flux60(*[west[:, f] for f in range(3, 6)], *[own[:, f] for f in range(3, 6)], u_sum)
    fields = jnp.concatenate(
        [east[:, :6], flux_theta[:, None], flux_w[:, None], west[:, 6:7], west[:, :6]], axis=1
    )
    return jnp.pad(fields.transpose(2, 0, 1), ((0, 0), (0, 0), (0, 128 - fields.shape[1])))


def advect_kernel(
    th_ref, th_lo, th_hi, w_ref, w_lo, w_hi, u_ref, v_ref, south, north, rim_ref, coef_ref, mixer_ref,
    sine_ref, weight_ref, decay_ref, start_ref,
    theta_out, star_out, spectral_out, edge_out, ends_out,
    th_s, w_s, u_s, v_s, new_s, modes_s, flow_s, carry_s, work_s,
):
    tile, tiles = pl.program_id(0), pl.num_programs(0)
    levels, rows, cols = th_ref.shape
    pairs = ((th_s, th_ref, th_lo, th_hi, 0), (w_s, w_ref, w_lo, w_hi, 3))

    @pl.loop(0, rows // 8)
    def _(group):
        at = pl.ds(pl.multiple_of(group * 8, 8), 8)
        for held, ref in ((th_s, th_ref), (w_s, w_ref)):
            held[pl.ds(group * 8 + 3, 8)] = jnp.swapaxes(ref[:, at, :], 0, 1)
        for held, ref in ((u_s, u_ref), (v_s, v_ref)):
            held[pl.ds(group * 8, 8)] = jnp.swapaxes(ref[:, at, :], 0, 1)

    @pl.when(tile == 0)
    def _():
        below = jnp.swapaxes(south[...], 0, 1)
        for held, _, _, _, field in pairs:
            held[0:3] = below[field : field + 3]
        v_before = below[6]
        th_q = [th_s[row] for row in range(6)]
        w_q = [w_s[row] for row in range(6)]
        flow_s[0] = flux60(*th_q, v_before * (time_step / 60.0))
        flow_s[1] = flux60(*w_q, (v_before + upper_of(v_before)) * (0.5 * time_step / 60.0))
        flow_s[2] = v_before
        carry_s[...] = jnp.zeros_like(carry_s)

    @pl.when(tile > 0)
    def _():
        for held, _, low, _, _ in pairs:
            held[0:3] = jnp.swapaxes(low[...], 0, 1)[5:8]

    @pl.when(tile == tiles - 1)
    def _():
        above = jnp.swapaxes(north[...], 0, 1)
        for held, _, _, _, field in pairs:
            held[rows + 3 : rows + 6] = above[field : field + 3]

    @pl.when(tile < tiles - 1)
    def _():
        for held, _, _, top, _ in pairs:
            held[rows + 3 : rows + 6] = jnp.swapaxes(top[...], 0, 1)[0:3]

    def along_x(field, before, after, speed, face):
        line = jnp.concatenate([before, field, after], axis=1)
        parts = [line[:, 126 + k : 126 + k + cols] for k in range(6)]
        flow = flux60(*parts, speed)
        return flow - jnp.concatenate([face, flow], axis=1)[:, 127 : 127 + cols]

    def along_z(field, ups, speed, inverse):
        low = lower_of(field)
        flow = flux60(lower_of(low), low, field, *ups, speed)
        return (flow - zero_below(flow)) * inverse

    def row(j, _):
        rim = rim_ref[j]
        coef = [wide(coef_ref[k], cols) for k in range(6)]
        theta, w, u, v = th_s[j + 3], w_s[j + 3], u_s[j], v_s[j]
        theta_ups = [upper_of(theta)]
        w_ups = [upper_of(w)]
        for _ in range(2):
            theta_ups.append(upper_of(theta_ups[-1]))
            w_ups.append(upper_of(w_ups[-1]))

        flow = flux60(*[th_s[j + 1 + k] for k in range(6)], v * (time_step / 60.0))
        change = flow - flow_s[0]
        flow_s[0] = flow
        change += along_x(
            theta, pltpu.roll(rim, 116, 1), rim, u * (time_step / 60.0), pltpu.roll(rim, 121, 1)
        )
        change += along_z(theta, theta_ups, w * coef[0], coef[1])
        new_s[j] = theta - change

        u_sum = (u + upper_of(u)) * (0.5 * time_step / 60.0)
        v_sum = (v + upper_of(v)) * (0.5 * time_step / 60.0)
        flow = flux60(*[w_s[j + 1 + k] for k in range(6)], v_sum)
        change = flow - flow_s[1]
        flow_s[1] = flow
        change += along_x(w, pltpu.roll(rim, 113, 1), pltpu.roll(rim, 125, 1), u_sum, pltpu.roll(rim, 120, 1))
        change += along_z(w, w_ups, (w + w_ups[0]) * coef[2], coef[3])
        star = w - change + (0.5 * time_step * buoyancy_gain) * (theta + theta_ups[0])
        star_out[row_of(j, levels), :] = star

        mass = coef[4] * star
        u_west = jnp.concatenate([pltpu.roll(rim, 119, 1), u], axis=1)[:, 127 : 127 + cols]
        source = (u - u_west + (v - flow_s[2])) * (1.0 / time_step) + (mass - zero_below(mass)) * coef[5]
        flow_s[2] = v
        modes_s[row_of(j, levels), :] = mix_levels(source, [wide(mixer_ref[k], cols) for k in range(levels)])
        return 0

    lax.fori_loop(0, rows, row, 0)

    @pl.loop(0, rows // 8)
    def _(group):
        at = pl.ds(pl.multiple_of(group * 8, 8), 8)
        theta_out[:, at, :] = jnp.swapaxes(new_s[pl.ds(group * 8, 8)], 0, 1)

    total = rows * levels
    spectral_out[...] = jnp.dot(modes_s[...], sine_ref[...], precision=high)
    here = pl.ds(pl.multiple_of(tile * total, total), total)
    edge_out[here, :] = spectral_out[:, 0:128]
    decay = decay_ref[...]
    carry_s[...] = forward_rows(
        lambda j: spectral_out[row_of(j, levels), :], decay, work_s, tile * rows, rows, carry_s[...]
    )

    @pl.when(tile == tiles - 1)
    def _():
        backward_rows(carry_s[...], decay, start_ref[...], work_s, ends_out, rows * tiles)

        @pl.loop(0, tiles)
        def _(step):
            at = pl.ds(pl.multiple_of(step * total, total), total)
            lane = lax.broadcasted_iota(jnp.int32, (total, 128), 1)
            near = jnp.where(lane == 0, edge_out[at, :], 0.0)
            edge_out[at, :] = near - jnp.dot(work_s[at, :], weight_ref[...], precision=high)


def advect(u_face, v_face, w_face, theta_field, sides, coef, mixer, tables):
    levels, rows, cols = theta_field.shape
    step = min(32, rows)
    tiles = rows // step
    south, north, rim = sides
    sine, weight, decay, start = tables
    block = pl.BlockSpec((levels, step, cols), lambda i: (0, i, 0))
    low = pl.BlockSpec((levels, 8, cols), lambda i: (0, jnp.maximum(i * (step // 8) - 1, 0), 0))
    top = pl.BlockSpec((levels, 8, cols), lambda i: (0, jnp.minimum((i + 1) * (step // 8), rows // 8 - 1), 0))

    def whole(value):
        return pl.BlockSpec(value.shape, lambda i: (0,) * value.ndim)

    flat = pl.BlockSpec((step * levels, cols), lambda i: (i, 0))
    big = jax.ShapeDtypeStruct((rows * levels, cols), jnp.float32)
    edge = jax.ShapeDtypeStruct((rows * levels, 128), jnp.float32)
    ends = jax.ShapeDtypeStruct((2, levels, cols), jnp.float32)

    def held(count):
        return pltpu.VMEM((count, levels, cols), jnp.float32)

    return pl.pallas_call(
        advect_kernel,
        grid=(tiles,),
        in_specs=[
            block, low, top, block, low, top, block, block, whole(south), whole(north),
            pl.BlockSpec((step, levels, 128), lambda i: (i, 0, 0)),
            whole(coef), whole(mixer), whole(sine), whole(weight), whole(decay), whole(start),
        ],
        out_specs=(block, flat, flat, whole(edge), whole(ends)),
        out_shape=(jax.ShapeDtypeStruct(theta_field.shape, jnp.float32), big, big, edge, ends),
        scratch_shapes=[
            held(step + 6), held(step + 6), held(step), held(step), held(step),
            pltpu.VMEM((step * levels, cols), jnp.float32),
            held(3),
            pltpu.VMEM((levels, cols), jnp.float32),
            pltpu.VMEM((rows * levels, cols), jnp.float32),
        ],
        compiler_params=pltpu.CompilerParams(vmem_limit_bytes=vmem_bytes),
        name="advect",
    )(
        theta_field, theta_field, theta_field, w_face, w_face, w_face, u_face, v_face, south, north, rim,
        coef, mixer, sine, weight, decay, start,
    )


def finish_kernel(
    free_ref, next_ref, line_ref, line_next, ends_ref, up_ref, down_ref, decay_ref, sine_ref, mixer_ref, coef_ref,
    star_ref, u_ref, v_ref, u_out, v_out, w_out, p_out, work_s, p_s, gx_s, gy_s, w_s,
):
    tile, tiles = pl.program_id(0), pl.num_programs(0)
    levels, rows, cols = u_ref.shape
    total = rows * levels
    decay = decay_ref[...]
    work_s[0:total, :] = free_ref[...]
    work_s[total : total + levels, :] = jnp.where(
        tile == tiles - 1, decay * free_ref[total - levels : total, :], next_ref[...]
    )

    def upward(j, carry):
        value = decay * carry
        work_s[row_of(j, levels), :] += value
        return value

    lax.fori_loop(0, rows + 1, upward, ends_ref[0] * up_ref[0], unroll=4)

    def downward(j, carry):
        work_s[row_of(rows - j, levels), :] += carry
        return decay * carry

    lax.fori_loop(0, rows + 1, downward, ends_ref[1] * down_ref[0], unroll=4)

    lane = lax.broadcasted_iota(jnp.int32, (total, 128), 1)
    work_s[0:total, 0:128] = jnp.where(lane == 0, line_ref[...], work_s[0:total, 0:128])
    work_s[total : total + levels, 0:128] = jnp.where(
        lane[:levels] == 0, line_next[...], work_s[total : total + levels, 0:128]
    )
    p_s[:, 0:cols] = jnp.dot(work_s[...], sine_ref[...], precision=high)
    mixer = [mixer_ref[k] for k in range(levels)]
    broad = [wide(tile_, cols) for tile_ in mixer]

    def physical(j, _):
        at = row_of(j, levels)
        p_s[at, 0:cols] = mix_levels(p_s[at, 0:cols], broad)
        return 0

    lax.fori_loop(0, rows + 1, physical, 0)
    spacing = wide(coef_ref[...], cols)
    top = lax.broadcasted_iota(jnp.int32, (levels, cols), 0) == levels - 1

    def gradient(j, _):
        at = row_of(j, levels)
        here = p_s[at, 0:cols]
        beside = mix_levels(pltpu.roll(line_ref[at, :], 127, 1), mixer)
        line = jnp.concatenate([here, beside], axis=1)
        gx_s[j] = time_step * (line[:, 1 : cols + 1] - here)
        gy_s[j] = time_step * (p_s[row_of(j + 1, levels), 0:cols] - here)
        above = jnp.where(top, 0.0, pltpu.roll(here, levels - 1, 0))
        w_s[j] = star_ref[at, :] - spacing * (above - here)
        return 0

    lax.fori_loop(0, rows, gradient, 0)

    @pl.loop(0, rows // 8)
    def _(group):
        at = pl.ds(pl.multiple_of(group * 8, 8), 8)
        some = pl.ds(group * 8, 8)
        u_out[:, at, :] = u_ref[:, at, :] - jnp.swapaxes(gx_s[some], 0, 1)
        v_out[:, at, :] = v_ref[:, at, :] - jnp.swapaxes(gy_s[some], 0, 1)
        w_out[:, at, :] = jnp.swapaxes(w_s[some], 0, 1)
        flat = pl.ds(pl.multiple_of(group * 8 * levels, 8 * levels), 8 * levels)
        p_out[:, at, :] = jnp.swapaxes(p_s[flat, 0:cols].reshape(8, levels, cols), 0, 1)


def finish(free, lines, ends, decay, sine, mixer, spacing, star, u_face, v_face):
    levels, rows, cols = u_face.shape
    step = min(32, rows)
    tiles = rows // step
    hop = power(decay, step)
    powers = [jnp.ones_like(decay)]
    for _ in range(tiles - 1):
        powers.append(powers[-1] * hop)
    powers = jnp.stack(powers)
    block = pl.BlockSpec((levels, step, cols), lambda i: (0, i, 0))
    flat = pl.BlockSpec((step * levels, cols), lambda i: (i, 0))
    ahead = pl.BlockSpec((levels, cols), lambda i: (jnp.minimum((i + 1) * step, rows - 1), 0))

    def whole(value):
        return pl.BlockSpec(value.shape, lambda i: (0,) * value.ndim)

    out = jax.ShapeDtypeStruct(u_face.shape, jnp.float32)

    def held(count):
        return pltpu.VMEM((count, levels, cols), jnp.float32)

    return pl.pallas_call(
        finish_kernel,
        grid=(tiles,),
        in_specs=[
            flat, ahead,
            pl.BlockSpec((step * levels, 128), lambda i: (i, 0)),
            pl.BlockSpec((levels, 128), lambda i: ((i + 1) * step, 0)),
            whole(ends),
            pl.BlockSpec((1, levels, cols), lambda i: (i, 0, 0)),
            pl.BlockSpec((1, levels, cols), lambda i: (tiles - 1 - i, 0, 0)),
            whole(decay), whole(sine), whole(mixer), whole(spacing), flat, block, block,
        ],
        out_specs=(block,) * 4,
        out_shape=(out,) * 4,
        scratch_shapes=[
            pltpu.VMEM(((step + 1) * levels, cols), jnp.float32),
            pltpu.VMEM(((step + 1) * levels, cols), jnp.float32),
            held(step), held(step), held(step),
        ],
        compiler_params=pltpu.CompilerParams(vmem_limit_bytes=vmem_bytes),
        name="finish",
    )(free, free, lines, lines, ends, powers, powers, decay, sine, mixer, spacing, star, u_face, v_face)


def tile_of(values):
    return jnp.broadcast_to(values[..., None], values.shape + (128,))


def rolled_mixer(matrix):
    levels = matrix.shape[0]
    index = np.arange(levels)
    return tile_of(jnp.stack([matrix[index, (index - shift) % levels] for shift in range(levels)]))


def per_device(u_face, v_face, w_face, theta_field, density, thickness):
    levels, rows, cols = theta_field.shape
    north, south, east, west = pack_sides(u_face, v_face, w_face, theta_field)
    south_halo, north_halo = from_behind(north, "gy", 1), from_behind(south, "gy", -1)
    west_halo, east_halo = from_behind(east, "gx", 1), from_behind(west, "gx", -1)

    face_density = (density + lift_level(density)) / 2.0
    face_spacing = (thickness + lift_level(thickness)) / 2.0
    forward, back, square = vertical_modes(density, thickness, face_density, face_spacing)
    mass = density * thickness
    coef = tile_of(
        jnp.stack(
            [
                face_density / 60.0,
                time_step / mass,
                lift_level(density) / 120.0,
                time_step / (face_density * face_spacing),
                face_density,
                1.0 / (mass * time_step),
            ]
        )
    )
    index = np.arange(cols)
    excess = (4.0 * np.sin(np.pi * index / (2 * cols)) ** 2).astype(np.float32) + square[:, None]
    decay = jnp.where(index[None, :] > 0, decay_of(excess), 0.0)
    start = -1.0 / (1.0 - decay * decay)
    ratio = power(decay, rows)
    sine = sine_matrix(cols)
    weight = edge_weights(cols)

    sides = (south_halo, north_halo, rim_lanes(west_halo, east_halo, west))
    theta_new, star, spectral, edge, free_ends = advect(
        u_face, v_face, w_face, theta_field, sides, coef, rolled_mixer(forward), (sine, weight, decay, start)
    )
    big = jax.ShapeDtypeStruct(spectral.shape, jnp.float32)
    scratch = [pltpu.VMEM(spectral.shape, jnp.float32)]
    params = pltpu.CompilerParams(vmem_limit_bytes=vmem_bytes)
    edge = pl.pallas_call(
        second_kernel,
        out_shape=jax.ShapeDtypeStruct(edge.shape, jnp.float32),
        scratch_shapes=scratch,
        compiler_params=params,
        name="edge_terms",
    )(decay, couple(free_ends, ratio), weight, edge)
    lines = separator_solve(edge, square, rows, cols)
    free, free_ends = pl.pallas_call(
        third_kernel,
        out_shape=(big, jax.ShapeDtypeStruct(free_ends.shape, jnp.float32)),
        scratch_shapes=scratch,
        compiler_params=params,
        name="second_solve",
    )(spectral, lines[: rows * levels], weight.T, decay, start)
    u_new, v_new, w_new, pressure = finish(
        free, lines, couple(free_ends, ratio), decay, sine, rolled_mixer(back.T),
        tile_of(time_step / face_spacing), star, u_face, v_face,
    )
    return (u_new, v_new, w_new, theta_new, pressure)


def solution(mesh):
    blocks = P(None, "gy", "gx")
    return jax.shard_map(
        per_device,
        mesh=mesh,
        in_specs=(blocks, blocks, blocks, blocks, P(), P()),
        out_specs=(blocks,) * 5,
        check_vma=False,
    )
```
